768 devices in a mesh: seq: 96 (over x, y_hi, z), fsdp: 8 (over y_lo, core).
Axes of the slice: x: 4, y: 8 (y_hi: 2, y_lo: 4; y = y_hi * 4 + y_lo), z: 12, core: 2. Of those that a mesh axis runs over, the one named last changes fastest.
Arguments:
- inputs: bfloat16 [3, 24576, 8192], P(None, 'seq', 'fsdp'), may hold values from -6 to 6
- grad_out: bfloat16 [24576, 8192], P('seq', 'fsdp'), may hold values from -6 to 6
- filters: bfloat16 [128, 8192], P('fsdp'), may hold values from -0.5 to 0.5
- short_weights: bfloat16 [3, 3, 8192], P(None, None, 'fsdp'), may hold values from -3.5 to 3.5
Outputs:
- grad_inputs: bfloat16 [3, 24576, 8192], P(None, 'seq', 'fsdp')
- grad_filters: float32 [128, 8192], P('fsdp')
- grad_short: float32 [3, 3, 8192], P(None, None, 'fsdp')
The draws below stay inside these ranges and needn't reach their ends.
All inputs are finite; a program needn't handle non-finite values.
Results may differ from the reference program's by a relative error of at most 0.0057.
Values may be sent and summed in bfloat16 or wider, within the bound.
A program may use at most 32 MiB of HBM per device.

```python
import jax
import jax.numpy as jnp
from jax import lax

WIDTH = 8192
FILTER_LEN = 128
SHORT_LEN = 3
SEQ_LEN = 24576


def block_levels(stream_key, dims, pieces, low, high):
    def one(dim, shards_of):
        heights = jax.random.uniform(jax.random.fold_in(jax.random.fold_in(stream_key, 6), dim), (shards_of,), jnp.float32, low / len(pieces), high / len(pieces))
        return jnp.repeat(jnp.exp(heights), dims[dim] // shards_of).reshape((-1,) + (1,) * (len(dims) - dim - 1))

    gain = one(*pieces[0])
    for cut in pieces[1:]:
        gain = gain * one(*cut)
    return gain


def noise(key, shape, spread, bound, shards=(), kind=jnp.bfloat16):
    drawn = jax.random.normal(key, shape, jnp.float32) * spread
    if len(shards) > 0:
        drawn = block_levels(key, shape, shards, -0.22, 0.18) * drawn
    return jnp.clip(drawn, min=-bound, max=bound).astype(kind)


def setup_inputs(seed: int = 0) -> dict:
    seeds = jax.random.split(jax.random.key(seed), 5)
    inputs = noise(seeds[0], (3, SEQ_LEN, WIDTH), 1.0, 6.0, ((1, 96), (2, 8)))
    grad_out = noise(seeds[1], (SEQ_LEN, WIDTH), 1.0, 6.0, ((0, 96), (1, 8)))
    filters = noise(seeds[2], (FILTER_LEN, WIDTH), FILTER_LEN ** -0.5, 0.5, ((0, 8),))
    short_weights = noise(seeds[3], (3, SHORT_LEN, WIDTH), SHORT_LEN ** -0.5, 3.5, ((2, 8),))
    return {"inputs": inputs, "grad_out": grad_out, "filters": filters, "short_weights": short_weights}


def reference(inputs, grad_out, filters, short_weights):
    block = 512 if WIDTH % 512 == 0 else WIDTH
    blocks = WIDTH // block
    lag = SHORT_LEN - 1
    length = inputs.shape[1]
    fft_len = length + FILTER_LEN

    def causal(signal, kernel):
        spectrum = jnp.fft.rfft(signal, fft_len, axis=0) * jnp.fft.rfft(kernel, fft_len, axis=0)
        return jnp.fft.irfft(spectrum, fft_len, axis=0)[:length]

    def one_block(first_col):
        source = lax.dynamic_slice_in_dim(inputs, first_col, block, 2).astype(jnp.float32)
        upstream = lax.dynamic_slice_in_dim(grad_out, first_col, block, 1).astype(jnp.float32)
        taps = lax.dynamic_slice_in_dim(filters, first_col, block, 1).astype(jnp.float32)
        weights = lax.dynamic_slice_in_dim(short_weights, first_col, block, 2).astype(jnp.float32)
        padded = jnp.pad(source, ((0, 0), (lag, 0), (0, 0)))
        shorts = weights[:, 0][:, None, :] * padded[:, lag:lag + length]
        for offset in range(1, SHORT_LEN):
            shorts = shorts + weights[:, offset][:, None, :] * padded[:, lag - offset:lag - offset + length]
        mixed_low = (shorts[1] * shorts[2]).astype(jnp.bfloat16)
        mixed = lax.optimization_barrier(mixed_low).astype(jnp.float32)
        long_out = causal(mixed, taps)
        grad_q = (upstream * long_out).astype(jnp.bfloat16)
        grad_long_low = (upstream * shorts[0]).astype(jnp.bfloat16)
        grad_long = lax.optimization_barrier(grad_long_low).astype(jnp.float32)
        grad_mixed = causal(grad_long[::-1], taps)[::-1]
        grad_k = (grad_mixed * shorts[2]).astype(jnp.bfloat16)
        grad_v = (grad_mixed * shorts[1]).astype(jnp.bfloat16)
        grads = lax.optimization_barrier(jnp.stack([grad_q, grad_k, grad_v])).astype(jnp.float32)
        trailing = jnp.pad(grads, ((0, 0), (0, lag), (0, 0)))
        grad_block = weights[:, 0][:, None, :] * trailing[:, 0:length]
        for offset in range(1, SHORT_LEN):
            grad_block = grad_block + weights[:, offset][:, None, :] * trailing[:, offset:offset + length]
        short_block = jnp.stack([jnp.sum(grads * padded[:, lag - offset:lag - offset + length], axis=1) for offset in range(SHORT_LEN)], axis=1)
        cross = jnp.fft.rfft(grad_long, fft_len, axis=0) * jnp.conj(jnp.fft.rfft(mixed, fft_len, axis=0))
        filt_block = jnp.fft.irfft(cross, fft_len, axis=0)[:FILTER_LEN]
        return grad_block.astype(jnp.bfloat16), filt_block.astype(jnp.float32), short_block.astype(jnp.float32)

    starts = (jnp.arange(blocks) * block).astype(jnp.int32)
    grad_all, filt_all, short_all = lax.map(one_block, starts)
    grad_inputs = jnp.moveaxis(grad_all, 0, 2).reshape(3, length, WIDTH)
    grad_filters = jnp.moveaxis(filt_all, 0, 1).reshape(FILTER_LEN, WIDTH)
    grad_short = jnp.moveaxis(short_all, 0, 2).reshape(3, SHORT_LEN, WIDTH)
    return grad_inputs, grad_filters, grad_short
```

```python
import functools

import jax
import jax.numpy as jnp
from jax import lax
from jax.experimental import pallas as pl
from jax.experimental.pallas import tpu as pltpu
from jax.sharding import PartitionSpec as P

FILTER_LEN = 128
SHORT_LEN = 3
NX, NYH, NZ = 4, 2, 12
GROUP = 16
LINK = jnp.float32
MESH = pl.DeviceIdType.MESH


def from_behind(block, axis, distance):
    devices = range(lax.axis_size(axis))
    route = [(i - distance, i) for i in devices if i - distance in devices]
    return lax.ppermute(block, axis, route)


def reduce_kernel(nf, part, filt_out, short_out, xs, xr, zs, zr, ys, yr, gs, ag, sx, rx, sz, rz, sy, ry, sg, rg, sh, rh, sa, ra):
    seq = lax.axis_index("seq")
    fs = lax.axis_index("fsdp")
    z = lax.rem(seq, NZ)
    yh = lax.rem(seq // NZ, NYH)
    x = seq // (NZ * NYH)
    groups = nf + 1
    cw = xs.shape[2]
    owner = z < groups

    def at(ax, ay, az):
        return (ax * NYH + ay) * NZ + az

    def around_x(d):
        return at(lax.rem(x + d, NX), yh, z)

    def around_z(d):
        return at(x, yh, lax.rem(z + d, NZ))

    across = at(x, 1 - yh, z)

    barrier = pltpu.get_barrier_semaphore()

    def greet(s, f):
        pl.semaphore_signal(barrier, inc=1, device_id=(s, f), device_id_type=MESH)

    for d in range(1, NX):
        greet(around_x(d), fs)
    for d in range(1, NZ):
        greet(around_z(d), fs)
    greet(across, fs)
    for f in range(nf):
        @pl.when(jnp.logical_or(z != fs, fs != f))
        def _(f=f):
            greet(at(x, yh, fs), f)

    for c in range(NX):
        xs[c] = part[:, c * cw:(c + 1) * cw].astype(xs.dtype)

    hearers = jnp.where(z < nf, jnp.where(z == fs, NZ - 1, NZ), 0)
    pl.semaphore_wait(barrier, NX - 1 + NZ - 1 + 1 + hearers)

    def remote(src, dst, ssem, rsem, s, f):
        return pltpu.make_async_remote_copy(
            src_ref=src, dst_ref=dst, send_sem=ssem, recv_sem=rsem, device_id=(s, f), device_id_type=MESH
        )

    def x_copy(d):
        return remote(xs.at[lax.rem(x + d, NX)], xr.at[d - 1], sx.at[d - 1], rx.at[d - 1], around_x(d), fs)

    for d in range(1, NX):
        x_copy(d).start()
    total = part[:, pl.ds(pl.multiple_of(x * cw, cw), cw)]
    for d in range(1, NX):
        x_copy(d).wait_recv()
        total = total + xr[d - 1].astype(jnp.float32)
    for g in range(groups):
        zs[g] = total[g * GROUP:(g + 1) * GROUP]

    def z_copy(d):
        return remote(zs.at[lax.rem(z + d, NZ)], zr.at[d - 1], sz.at[d - 1], rz.at[d - 1], around_z(d), fs)

    for d in range(1, NZ):
        @pl.when(lax.rem(z + d, NZ) < groups)
        def _(d=d):
            z_copy(d).start()

    def y_copy():
        return remote(ys, yr, sy, ry, across, fs)

    def g_copy(d, f):
        return remote(gs, ag.at[x, fs], sg.at[d], rg.at[fs], around_z(d), f)

    def g_landing(f):
        return remote(ag.at[x, f], ag.at[x, f], sg.at[0], rg.at[f], across, fs)

    def h_copy(d):
        return remote(ag.at[x, nf], ag.at[x, nf], sh.at[d - 1], rh, around_z(d), fs)

    @pl.when(owner)
    def _():
        total = zs[z]
        for d in range(1, NZ):
            z_copy(d).wait_recv()
            total = total + zr[d - 1].astype(jnp.float32)
        ys[...] = total.astype(ys.dtype)
        y_copy().start()
        y_copy().wait_recv()
        piece = (total + yr[...].astype(jnp.float32)).astype(ag.dtype)
        y_copy().wait_send()

        @pl.when(z < nf)
        def _():
            gs[...] = piece

            @pl.when(z == fs)
            def _():
                ag[x, fs] = piece

            for d in range(NZ):
                @pl.when(jnp.logical_or(d != 0, z != fs))
                def _(d=d):
                    g_copy(d, z).start()

        @pl.when(z == nf)
        def _():
            ag[x, nf] = piece
            for d in range(1, NZ):
                h_copy(d).start()

    for f in range(nf):
        @pl.when(jnp.logical_or(z != fs, fs != f))
        def _(f=f):
            g_landing(f).wait_recv()

    @pl.when(z != nf)
    def _():
        h_copy(1).wait_recv()

    def a_copy(d):
        return remote(ag.at[x], ag.at[x], sa.at[d - 1], ra.at[d - 1], around_x(d), fs)

    def a_landing(d):
        back = lax.rem(x + NX - d, NX)
        return remote(ag.at[back], ag.at[back], sa.at[d - 1], ra.at[d - 1], around_x(d), fs)

    for d in range(1, NX):
        x_copy(d).wait_send()
    for d in range(1, NX):
        a_copy(d).start()
    for d in range(1, NX):
        a_landing(d).wait_recv()
    for c in range(NX):
        for f in range(nf):
            lo = f * NX * cw + c * cw
            filt_out[:, lo:lo + cw] = ag[c, f].astype(jnp.float32)
        short_out[:, c * cw:(c + 1) * cw] = ag[c, nf].astype(jnp.float32)

    for d in range(1, NX):
        a_copy(d).wait_send()
    for d in range(1, NZ):
        @pl.when(lax.rem(z + d, NZ) < groups)
        def _(d=d):
            z_copy(d).wait_send()

    @pl.when(z < nf)
    def _():
        for d in range(NZ):
            @pl.when(jnp.logical_or(d != 0, z != fs))
            def _(d=d):
                g_copy(d, z).wait_send()

    @pl.when(z == nf)
    def _():
        for d in range(1, NZ):
            h_copy(d).wait_send()


def reduced(part, nf):
    rows, width = part.shape
    cw = width // NX
    dma = pltpu.SemaphoreType.DMA
    vm = pl.BlockSpec(memory_space=pltpu.VMEM)
    return pl.pallas_call(
        functools.partial(reduce_kernel, nf),
        out_shape=(
            jax.ShapeDtypeStruct((GROUP, nf * width), jnp.float32),
            jax.ShapeDtypeStruct((GROUP, width), jnp.float32),
        ),
        in_specs=[vm],
        out_specs=(vm, vm),
        scratch_shapes=[
            pltpu.VMEM((NX, rows, cw), LINK),
            pltpu.VMEM((NX - 1, rows, cw), LINK),
            pltpu.VMEM((NZ, GROUP, cw), LINK),
            pltpu.VMEM((NZ - 1, GROUP, cw), LINK),
            pltpu.VMEM((GROUP, cw), LINK),
            pltpu.VMEM((GROUP, cw), LINK),
            pltpu.VMEM((GROUP, cw), LINK),
            pltpu.VMEM((NX, nf + 1, GROUP, cw), LINK),
            dma((NX - 1,)), dma((NX - 1,)),
            dma((NZ - 1,)), dma((NZ - 1,)),
            dma, dma,
            dma((NZ,)), dma((nf,)),
            dma((NZ - 1,)), dma,
            dma((NX - 1,)), dma((NX - 1,)),
        ],
        compiler_params=pltpu.CompilerParams(
            collective_id=0, has_side_effects=True, vmem_limit_bytes=40 * 1024 * 1024
        ),
    )(part)


def depthwise(signal, kernel):
    result = lax.conv_general_dilated(
        signal[None],
        kernel[:, None, :],
        (1,),
        "VALID",
        dimension_numbers=("NWC", "WIO", "NWC"),
        feature_group_count=signal.shape[1],
        preferred_element_type=jnp.float32,
    )
    return result[0]


def short_forward(padded, weights, count):
    lag = weights.shape[1] - 1
    result = weights[:, 0][:, None, :] * padded[:, lag : lag + count]
    for offset in range(1, weights.shape[1]):
        result = (
            result + weights[:, offset][:, None, :] * padded[:, lag - offset : lag - offset + count]
        )
    return result


def short_backward(trailing, weights, count):
    result = weights[:, 0][:, None, :] * trailing[:, 0:count]
    for offset in range(1, weights.shape[1]):
        result = result + weights[:, offset][:, None, :] * trailing[:, offset : offset + count]
    return result


def upper_rows(piece):
    return from_behind(piece, "seq", -1)


def local(inputs, grad_out, filters, short_weights):
    rows = inputs.shape[1]
    nf = lax.axis_size("fsdp")
    lag = SHORT_LEN - 1
    reach = FILTER_LEN - 1
    taps = lax.all_to_all(filters, "fsdp", split_axis=1, concat_axis=0, tiled=True)
    weights = short_weights.astype(jnp.float32)
    span = reach + lag
    outgoing = jnp.concatenate(
        [inputs[0, rows - lag :], inputs[1, rows - span :], inputs[2, rows - span :]], axis=0
    )
    incoming = from_behind(outgoing, "seq", 1)
    prior_q = incoming[:lag]
    prior_k = incoming[lag : lag + span]
    prior_v = incoming[lag + span :]
    earlier = jnp.stack([prior_q, prior_k[span - lag :], prior_v[span - lag :]])
    padded = jnp.concatenate([earlier, inputs], axis=1).astype(jnp.float32)
    shorts = short_forward(padded, weights, rows)
    mixed = (shorts[1] * shorts[2]).astype(jnp.bfloat16)
    prior_shorts = short_forward(
        jnp.stack([prior_k, prior_v]).astype(jnp.float32), weights[1:], reach
    )
    mixed_below = (prior_shorts[0] * prior_shorts[1]).astype(jnp.bfloat16)
    mixed_ext = jnp.concatenate([mixed_below, mixed], axis=0)
    long_out = depthwise(mixed_ext, taps[::-1])
    upstream = grad_out.astype(jnp.float32)
    grad_q = (upstream * long_out).astype(jnp.bfloat16)
    grad_long = (upstream * shorts[0]).astype(jnp.bfloat16)
    following = upper_rows(grad_long[:reach])
    grad_mixed = depthwise(jnp.concatenate([grad_long, following], axis=0), taps)
    grad_k = (grad_mixed * shorts[2]).astype(jnp.bfloat16)
    grad_v = (grad_mixed * shorts[1]).astype(jnp.bfloat16)
    stacked = jnp.stack([grad_q, grad_k, grad_v])
    upper = upper_rows(stacked[:, :lag])
    trailing = jnp.concatenate([stacked, upper], axis=1).astype(jnp.float32)
    grad_inputs = short_backward(trailing, weights, rows).astype(jnp.bfloat16)
    stacked_wide = stacked.astype(jnp.float32)
    short_terms = jnp.stack(
        [
            jnp.sum(stacked_wide * padded[:, lag - offset : lag - offset + rows], axis=1)
            for offset in range(SHORT_LEN)
        ],
        axis=1,
    )
    filter_terms = depthwise(mixed_ext, grad_long)[::-1]
    width = inputs.shape[2]
    spare = jnp.zeros((GROUP - 9, width), jnp.float32)
    part = jnp.concatenate([filter_terms, short_terms.reshape(9, width), spare], axis=0)
    grad_filters, short_rows = reduced(part, nf)
    grad_short = short_rows[:9].reshape(3, SHORT_LEN, width)
    return (grad_inputs, grad_filters, grad_short)


def solution(mesh):
    placed = (P(None, "seq", "fsdp"), P("seq", "fsdp"), P("fsdp", None), P(None, None, "fsdp"))
    return jax.shard_map(
        local,
        mesh=mesh,
        in_specs=placed,
        out_specs=(P(None, "seq", "fsdp"), P("fsdp", None), P(None, None, "fsdp")),
        check_vma=False,
    )
```

```python
import functools

import jax
import jax.numpy as jnp
import numpy as np
from jax import lax
from jax.experimental import pallas as pl
from jax.experimental.pallas import tpu as pltpu
from jax.sharding import PartitionSpec as P

FILTER_LEN = 128
SHORT_LEN = 3
NX, NYH, NZ = 4, 2, 12
GROUP = 16
LAG = 8
BLOCK = 32
LINK = jnp.float32
MESH = pl.DeviceIdType.MESH
F32, BF16 = jnp.float32, jnp.bfloat16


def basis(length):
    k = np.arange(length // 2, dtype=np.int64)[:, None]
    t = np.arange(length, dtype=np.int64)[None, :]
    angle = np.pi * (((2 * k + 1) * t) % (2 * length)) / length
    return np.concatenate([np.cos(angle), -np.sin(angle)], axis=0)


def split(matrix):
    high = matrix.astype(jnp.bfloat16)
    low = (matrix - high.astype(np.float64)).astype(jnp.bfloat16)
    return high, low


def dot(a, b):
    return jnp.dot(a, b, preferred_element_type=F32)


def fused_kernel(
    nf, inp, go, filt, sw, dh, dl, ih, il,
    ginp, gfilt, gshort,
    pad, wts, kv, mext, gext, taps, ghead, trail, gspec, mspec, stage, zh, zl,
    etail, etail_in, ehead, ehead_in, egrad, egrad_in,
    part, xs, xr, zs, zr, ys, yr, gs, ag,
    s_fil, r_fil, s_edge, r_edge, s_mix, r_mix, s_gl, r_gl,
    sx, rx, sxs, rxs, sz, rz, sy, ry, sg, rg, sh, rh, sa, ra,
):
    seq = lax.axis_index("seq")
    fs = lax.axis_index("fsdp")
    last = NX * NYH * NZ - 1
    z = lax.rem(seq, NZ)
    yh = lax.rem(seq // NZ, NYH)
    x = seq // (NZ * NYH)
    groups = nf + 1
    rows, width = go.shape
    cw = width // NX
    reach = FILTER_LEN
    size = rows + reach
    half = size // 2
    taps_n = nf * GROUP
    assert taps_n == reach
    owner = z < groups
    has_prev = seq > 0
    has_next = seq < last
    scale = 2.0 / size

    def at(ax, ay, az):
        return (ax * NYH + ay) * NZ + az

    def around_x(d):
        return at(lax.rem(x + d, NX), yh, z)

    def around_z(d):
        return at(x, yh, lax.rem(z + d, NZ))

    def around_f(d):
        return lax.rem(fs + d, nf)

    def lanes(c):
        return pl.ds(pl.multiple_of(c * cw, cw), cw)

    across = at(x, 1 - yh, z)

    def remote(src, dst, ssem, rsem, s, f):
        return pltpu.make_async_remote_copy(
            src_ref=src, dst_ref=dst, send_sem=ssem, recv_sem=rsem, device_id=(s, f), device_id_type=MESH
        )

    barrier = pltpu.get_barrier_semaphore()

    def greet(s, f):
        pl.semaphore_signal(barrier, inc=1, device_id=(s, f), device_id_type=MESH)

    pl.when(has_prev)(lambda: greet(seq - 1, fs))
    pl.when(has_next)(lambda: greet(seq + 1, fs))
    for d in range(1, nf):
        greet(seq, around_f(d))
    for d in range(1, NX):
        greet(around_x(d), fs)
    for d in range(1, NZ):
        greet(around_z(d), fs)
    greet(across, fs)
    for f in range(nf):
        pl.when(jnp.logical_or(z != fs, fs != f))(lambda f=f: greet(at(x, yh, fs), f))

    stage[...] = jnp.zeros_like(stage)
    for i in range(3):
        stage[2 * i:2 * i + 2] = inp[i, rows - GROUP:rows].astype(F32)[GROUP - 2:GROUP]
    etail[...] = stage[...].astype(BF16)
    stage[...] = jnp.zeros_like(stage)
    stage[0:2] = inp[0, 0:GROUP].astype(F32)[0:2]
    stage[2:4] = go[0:GROUP].astype(F32)[0:2]
    ehead[...] = stage[...].astype(BF16)
    for i in range(3):
        wts[3 * i:3 * i + 3] = sw[i].astype(F32)

    def tap(i, j, c):
        return wts[3 * i + j:3 * i + j + 1, lanes(c)]

    def short(i, c, lo, n):
        total = tap(i, 0, c) * pad[c, i, LAG + lo:LAG + lo + n]
        for j in range(1, SHORT_LEN):
            total = total + tap(i, j, c) * pad[c, i, LAG + lo - j:LAG + lo - j + n]
        return total

    def mix(c, lo):
        for b in range(lo, lo + reach, BLOCK):
            k = short(1, c, b, BLOCK)
            v = short(2, c, b, BLOCK)
            kv[c, 0, b:b + BLOCK] = k
            kv[c, 1, b:b + BLOCK] = v
            mext[c, reach + b:reach + b + BLOCK] = (k * v).astype(BF16)

    def tail(c, carry):
        for i in range(3):
            pad[c, i, 0:LAG] = jnp.zeros((LAG, cw), F32)
            for b in range(0, rows, BLOCK):
                pad[c, i, LAG + b:LAG + b + BLOCK] = inp[i, b:b + BLOCK, lanes(c)].astype(F32)
        mix(c, rows - reach)
        for b in range(0, reach, BLOCK):
            ghead[c, b:b + BLOCK] = (go[b:b + BLOCK, lanes(c)].astype(F32) * short(0, c, b, BLOCK)).astype(BF16)
        return carry

    lax.fori_loop(0, NX, tail, 0)

    hearers = jnp.where(z < nf, jnp.where(z == fs, NZ - 1, NZ), 0)
    ends = jnp.where(has_prev, 1, 0) + jnp.where(has_next, 1, 0)
    pl.semaphore_wait(barrier, NX - 1 + NZ - 1 + 1 + nf - 1 + hearers + ends)

    def tail_edge():
        return remote(etail, etail_in, s_edge.at[0], r_edge.at[0], seq + 1, fs)

    def head_edge():
        return remote(ehead, ehead_in, s_edge.at[1], r_edge.at[1], seq - 1, fs)

    def grad_edge():
        return remote(egrad, egrad_in, s_edge.at[2], r_edge.at[2], seq - 1, fs)

    def mix_copy(c):
        return remote(mext.at[c, pl.ds(rows, reach)], mext.at[c, pl.ds(0, reach)], s_mix.at[c], r_mix.at[c], seq + 1, fs)

    def long_copy(c):
        return remote(ghead.at[c], gext.at[c, pl.ds(rows, reach)], s_gl.at[c], r_gl.at[c], seq - 1, fs)

    def filt_copy(d):
        f = around_f(d)
        src = filt.at[:, pl.ds(pl.multiple_of(f * width, width), width)]
        dst = taps.at[pl.ds(pl.multiple_of(fs * GROUP, GROUP), GROUP)]
        return remote(src, dst, s_fil.at[d - 1], r_fil.at[d - 1], seq, f)

    @pl.when(has_next)
    def _():
        tail_edge().start()
        for d in range(NX):
            mix_copy(lax.rem(x + 1 + d, NX)).start()

    @pl.when(has_prev)
    def _():
        head_edge().start()
        for d in range(NX):
            long_copy(lax.rem(x + 1 + d, NX)).start()

    for d in range(1, nf):
        filt_copy(d).start()
    taps[pl.ds(pl.multiple_of(fs * GROUP, GROUP), GROUP)] = filt[:, pl.ds(pl.multiple_of(fs * width, width), width)]

    @pl.when(has_prev)
    def _():
        tail_edge().wait_recv()

    @pl.when(jnp.logical_not(has_prev))
    def _():
        etail_in[...] = jnp.zeros_like(etail_in)
        for c in range(NX):
            mext[c, 0:reach] = jnp.zeros((reach, cw), BF16)

    @pl.when(has_next)
    def _():
        head_edge().wait_recv()

    @pl.when(jnp.logical_not(has_next))
    def _():
        ehead_in[...] = jnp.zeros_like(ehead_in)
        egrad_in[...] = jnp.zeros_like(egrad_in)
        for c in range(NX):
            gext[c, rows:size] = jnp.zeros((reach, cw), BF16)

    def rest(c, carry):
        edge = etail_in[:, lanes(c)].astype(F32)
        for i in range(3):
            pad[c, i, LAG - 2:LAG] = edge[2 * i:2 * i + 2]
        mix(c, 0)
        for b in range(0, rows, BLOCK):
            gext[c, b:b + BLOCK] = (go[b:b + BLOCK, lanes(c)].astype(F32) * short(0, c, b, BLOCK)).astype(BF16)
        return carry

    lax.fori_loop(0, NX, rest, 0)

    def forward(signal, lo, n):
        return dot(dh[:, lo:lo + n], signal) + dot(dl[:, lo:lo + n], signal)

    def backward(c, lo, n):
        return scale * (
            dot(ih[lo:lo + n], zh[...]) + (dot(ih[lo:lo + n], zl[...]) + dot(il[lo:lo + n], zh[...]))
        )

    def put(lo, value):
        n = value.shape[0]
        high = value.astype(BF16)
        zh[lo:lo + n] = high
        zl[lo:lo + n] = (value - high.astype(F32)).astype(BF16)

    def product(a, b, c):
        for lo in range(0, half, BLOCK):
            ar, ai = a[c, lo:lo + BLOCK], a[c, half + lo:half + lo + BLOCK]
            br, bi = b[c, lo:lo + BLOCK], b[c, half + lo:half + lo + BLOCK]
            put(lo, ar * br + ai * bi)
            put(half + lo, ai * br - ar * bi)

    def x_copy(d):
        src = (part if LINK == F32 else xs).at[lax.rem(x + 1 + d, NX), pl.ds(0, taps_n)]
        return remote(src, xr.at[d, pl.ds(0, taps_n)], sx.at[d], rx.at[d], around_x(1 + d), fs)

    def xs_copy(d):
        src = (part if LINK == F32 else xs).at[lax.rem(x + 1 + d, NX), pl.ds(taps_n, GROUP)]
        return remote(src, xr.at[d, pl.ds(taps_n, GROUP)], sxs.at[d], rxs.at[d], around_x(1 + d), fs)

    def cross(d, carry):
        c = lax.rem(x + 1 + d, NX)

        @pl.when(has_prev)
        def _():
            mix_copy(c).wait_recv()

        gspec[c] = forward(gext[c, 0:rows], 0, rows)
        mspec[c] = forward(mext[c], 0, size)
        product(gspec, mspec, c)
        terms = -backward(c, rows, reach)
        part[c, 0:taps_n] = terms
        if LINK != F32:
            xs[c, 0:taps_n] = terms.astype(LINK)

        @pl.when(d < NX - 1)
        def _():
            x_copy(d).start()

        return carry

    lax.fori_loop(0, NX, cross, 0)

    for d in range(1, nf):
        filt_copy(d).wait_recv()

    def outputs(d, carry):
        c = lax.rem(x + 1 + d, NX)
        spectrum = forward(taps[:, lanes(c)], 0, reach)

        @pl.when(has_next)
        def _():
            long_copy(c).wait_recv()
            block = gext[c, rows:rows + GROUP].astype(F32)
            edge = ehead_in[:, lanes(c)].astype(F32)
            before = pad[c, 0, LAG + rows - 2:LAG + rows]
            first = tap(0, 0, c) * edge[0:1] + tap(0, 1, c) * before[1:2] + tap(0, 2, c) * before[0:1]
            second = tap(0, 0, c) * edge[1:2] + tap(0, 1, c) * edge[0:1] + tap(0, 2, c) * before[1:2]
            row = lax.broadcasted_iota(jnp.int32, (GROUP, cw), 0)
            block = jnp.where(row == 0, edge[2:3] * first, block)
            block = jnp.where(row == 1, edge[3:4] * second, block)
            gext[c, rows:rows + GROUP] = block.astype(BF16)

        fr, fi = spectrum[:half], spectrum[half:]
        for lo in range(0, half, BLOCK):
            ar, ai = mspec[c, lo:lo + BLOCK], mspec[c, half + lo:half + lo + BLOCK]
            br, bi = fr[lo:lo + BLOCK], fi[lo:lo + BLOCK]
            put(lo, ar * br - ai * bi)
            put(half + lo, ar * bi + ai * br)
        long_out = backward(c, reach, rows)
        trail[c, 0, 0:rows] = (go[:, lanes(c)].astype(F32) * long_out).astype(BF16).astype(F32)
        gspec[c] = gspec[c] + forward(gext[c, rows:size], rows, reach)
        for lo in range(0, half, BLOCK):
            ar, ai = gspec[c, lo:lo + BLOCK], gspec[c, half + lo:half + lo + BLOCK]
            br, bi = fr[lo:lo + BLOCK], fi[lo:lo + BLOCK]
            put(lo, ar * br + ai * bi)
            put(half + lo, ai * br - ar * bi)
        grad_mixed = backward(c, 0, rows)
        trail[c, 1, 0:rows] = (grad_mixed * kv[c, 1]).astype(BF16).astype(F32)
        trail[c, 2, 0:rows] = (grad_mixed * kv[c, 0]).astype(BF16).astype(F32)
        part[c, taps_n:taps_n + GROUP] = jnp.zeros((GROUP, cw), F32)
        for i in range(3):
            sums = [jnp.zeros((8, cw), F32)] * SHORT_LEN
            for b in range(0, rows, BLOCK):
                grads = trail[c, i, b:b + BLOCK]
                for j in range(SHORT_LEN):
                    terms = grads * pad[c, i, LAG + b - j:LAG + b - j + BLOCK]
                    sums[j] = sums[j] + jnp.sum(terms.reshape(BLOCK // 8, 8, cw), axis=0)
            for j in range(SHORT_LEN):
                r = taps_n + 3 * i + j
                part[c, r:r + 1] = jnp.sum(sums[j], axis=0, keepdims=True)
        if LINK != F32:
            xs[c, taps_n:taps_n + GROUP] = part[c, taps_n:taps_n + GROUP].astype(LINK)
        for i in range(3):
            stage[2 * i:2 * i + 2, lanes(c)] = trail[c, i, 0:2]

        @pl.when(d < NX - 1)
        def _():
            xs_copy(d).start()

        return carry

    stage[...] = jnp.zeros_like(stage)
    lax.fori_loop(0, NX, outputs, 0)
    egrad[...] = stage[...].astype(BF16)

    @pl.when(has_prev)
    def _():
        grad_edge().start()

    def z_copy(d):
        return remote(zs.at[lax.rem(z + d, NZ)], zr.at[d - 1], sz.at[d - 1], rz.at[d - 1], around_z(d), fs)

    def y_copy():
        return remote(ys, yr, sy, ry, across, fs)

    def g_copy(d, f):
        return remote(gs, ag.at[x, fs], sg.at[d], rg.at[fs], around_z(d), f)

    def g_landing(f):
        return remote(ag.at[x, f], ag.at[x, f], sg.at[0], rg.at[f], across, fs)

    def h_copy(d):
        return remote(ag.at[x, nf], ag.at[x, nf], sh.at[d - 1], rh, around_z(d), fs)

    def a_copy(d, g):
        return remote(ag.at[x, g], ag.at[x, g], sa.at[d - 1, g], ra.at[d - 1, g], around_x(d), fs)

    def a_landing(d, g):
        back = lax.rem(x + NX - d, NX)
        return remote(ag.at[back, g], ag.at[back, g], sa.at[d - 1, g], ra.at[d - 1, g], around_x(d), fs)

    for d in range(NX - 1):
        x_copy(d).wait_recv()
        xs_copy(d).wait_recv()
    for d in range(1, NZ + 1):
        g = lax.rem(z + d, NZ)

        @pl.when(g < groups)
        def _(d=d, g=g):
            here = pl.ds(pl.multiple_of(g * GROUP, GROUP), GROUP)
            total = part[x, here]
            for e in range(NX - 1):
                total = total + xr[e, here].astype(F32)
            zs[g] = total.astype(zs.dtype)
            if d < NZ:
                z_copy(d).start()

    @pl.when(has_next)
    def _():
        grad_edge().wait_recv()

    def finish(c, carry):
        edge = egrad_in[:, lanes(c)].astype(F32)
        for i in range(3):
            trail[c, i, rows:rows + 2] = edge[2 * i:2 * i + 2]
            for b in range(0, rows, BLOCK):
                total = tap(i, 0, c) * trail[c, i, b:b + BLOCK]
                for j in range(1, SHORT_LEN):
                    total = total + tap(i, j, c) * trail[c, i, b + j:b + j + BLOCK]
                ginp[i, b:b + BLOCK, lanes(c)] = total.astype(BF16)
        return carry

    lax.fori_loop(0, NX, finish, 0)

    @pl.when(owner)
    def _():
        total = zs[z].astype(F32)
        for d in range(1, NZ):
            z_copy(d).wait_recv()
            total = total + zr[d - 1].astype(F32)
        ys[...] = total.astype(ys.dtype)
        y_copy().start()
        y_copy().wait_recv()
        piece = (total + yr[...].astype(F32)).astype(ag.dtype)
        y_copy().wait_send()

        @pl.when(z < nf)
        def _():
            gs[...] = piece

            @pl.when(z == fs)
            def _():
                ag[x, fs] = piece

            for d in range(NZ):
                pl.when(jnp.logical_or(d != 0, z != fs))(lambda d=d: g_copy(d, z).start())

        @pl.when(z == nf)
        def _():
            ag[x, nf] = piece
            for d in range(1, NZ):
                h_copy(d).start()

    for g in range(groups):
        if g < nf:
            pl.when(jnp.logical_or(z != fs, fs != g))(lambda g=g: g_landing(g).wait_recv())
        else:
            pl.when(z != nf)(lambda: h_copy(1).wait_recv())
        for d in range(1, NX):
            a_copy(d, g).start()

    def deliver(c, g):
        if g < nf:
            gfilt[:, pl.ds(pl.multiple_of(g * width + c * cw, cw), cw)] = ag[c, g].astype(F32)
        else:
            for i in range(3):
                gshort[i, :, lanes(c)] = ag[c, g].astype(F32)[3 * i:3 * i + 3]

    for g in range(groups):
        deliver(x, g)
    for g in range(groups):
        for d in range(1, NX):
            a_landing(d, g).wait_recv()
            deliver(lax.rem(x + NX - d, NX), g)

    for d in range(1, nf):
        filt_copy(d).wait_send()
    for d in range(NX - 1):
        x_copy(d).wait_send()
        xs_copy(d).wait_send()

    @pl.when(has_next)
    def _():
        tail_edge().wait_send()
        for c in range(NX):
            mix_copy(c).wait_send()

    @pl.when(has_prev)
    def _():
        head_edge().wait_send()
        grad_edge().wait_send()
        for c in range(NX):
            long_copy(c).wait_send()

    for d in range(1, NZ):
        pl.when(lax.rem(z + d, NZ) < groups)(lambda d=d: z_copy(d).wait_send())

    @pl.when(z < nf)
    def _():
        for d in range(NZ):
            pl.when(jnp.logical_or(d != 0, z != fs))(lambda d=d: g_copy(d, z).wait_send())

    @pl.when(z == nf)
    def _():
        for d in range(1, NZ):
            h_copy(d).wait_send()

    for g in range(groups):
        for d in range(1, NX):
            a_copy(d, g).wait_send()


def local(inputs, grad_out, filters, short_weights):
    rows, width = grad_out.shape
    nf = lax.axis_size("fsdp")
    cw = width // NX
    size = rows + FILTER_LEN
    matrix = basis(size)
    dh, dl = split(matrix)
    ih, il = (np.ascontiguousarray(m.T) for m in (dh, dl))
    part_rows = (nf + 1) * GROUP
    dma = pltpu.SemaphoreType.DMA
    vm = pl.BlockSpec(memory_space=pltpu.VMEM)
    return pl.pallas_call(
        functools.partial(fused_kernel, nf),
        out_shape=(
            jax.ShapeDtypeStruct(inputs.shape, BF16),
            jax.ShapeDtypeStruct((GROUP, nf * width), F32),
            jax.ShapeDtypeStruct((3, SHORT_LEN, width), F32),
        ),
        in_specs=[vm] * 8,
        out_specs=(vm,) * 3,
        scratch_shapes=[
            pltpu.VMEM((NX, 3, LAG + rows, cw), F32),
            pltpu.VMEM((GROUP, width), F32),
            pltpu.VMEM((NX, 2, rows, cw), F32),
            pltpu.VMEM((NX, size, cw), BF16),
            pltpu.VMEM((NX, size, cw), BF16),
            pltpu.VMEM((FILTER_LEN, width), BF16),
            pltpu.VMEM((NX, FILTER_LEN, cw), BF16),
            pltpu.VMEM((NX, 3, rows + LAG, cw), F32),
            pltpu.VMEM((NX, size, cw), F32),
            pltpu.VMEM((NX, size, cw), F32),
            pltpu.VMEM((GROUP, width), F32),
            pltpu.VMEM((size, cw), BF16),
            pltpu.VMEM((size, cw), BF16),
            *[pltpu.VMEM((GROUP, width), BF16)] * 6,
            pltpu.VMEM((NX, part_rows, cw), F32),
            pltpu.VMEM((NX, part_rows, cw), LINK),
            pltpu.VMEM((NX - 1, part_rows, cw), LINK),
            pltpu.VMEM((NZ, GROUP, cw), LINK),
            pltpu.VMEM((NZ - 1, GROUP, cw), LINK),
            pltpu.VMEM((GROUP, cw), LINK),
            pltpu.VMEM((GROUP, cw), LINK),
            pltpu.VMEM((GROUP, cw), LINK),
            pltpu.VMEM((NX, nf + 1, GROUP, cw), LINK),
            dma((nf - 1,)), dma((nf - 1,)),
            dma((3,)), dma((3,)),
            dma((NX,)), dma((NX,)),
            dma((NX,)), dma((NX,)),
            dma((NX - 1,)), dma((NX - 1,)),
            dma((NX - 1,)), dma((NX - 1,)),
            dma((NZ - 1,)), dma((NZ - 1,)),
            dma, dma,
            dma((NZ,)), dma((nf,)),
            dma((NZ - 1,)), dma,
            dma((NX - 1, nf + 1)), dma((NX - 1, nf + 1)),
        ],
        compiler_params=pltpu.CompilerParams(
            collective_id=0, has_side_effects=True, vmem_limit_bytes=56 * 1024 * 1024
        ),
    )(inputs, grad_out, filters, short_weights, dh, dl, ih, il)


def solution(mesh):
    placed = (P(None, "seq", "fsdp"), P("seq", "fsdp"), P("fsdp", None), P(None, None, "fsdp"))
    return jax.shard_map(
        local,
        mesh=mesh,
        in_specs=placed,
        out_specs=(P(None, "seq", "fsdp"), P("fsdp", None), P(None, None, "fsdp")),
        check_vma=False,
    )
```

```python
import functools

import jax
import jax.numpy as jnp
import numpy as np
from jax import lax
from jax.experimental import pallas as pl
from jax.experimental.pallas import tpu as pltpu
from jax.sharding import PartitionSpec as P

FILTER_LEN = 128
SHORT_LEN = 3
NX, NYH, NZ = 4, 2, 12
GROUP = 16
LAG = 8
BLOCK = 32
LINK = jnp.bfloat16
MESH = pl.DeviceIdType.MESH
F32, BF16 = jnp.float32, jnp.bfloat16


def basis(length):
    k = np.arange(length // 2, dtype=np.int64)[:, None]
    t = np.arange(length, dtype=np.int64)[None, :]
    angle = np.pi * (((2 * k + 1) * t) % (2 * length)) / length
    return np.concatenate([np.cos(angle), -np.sin(angle)], axis=0)


def split(matrix):
    high = matrix.astype(jnp.bfloat16)
    low = (matrix - high.astype(np.float64)).astype(jnp.bfloat16)
    return high, low


def dot(a, b):
    return jnp.dot(a, b, preferred_element_type=F32)


def fused_kernel(
    nf, inp_in, go_in, filt_in, sw_in, fwd_in, bwd_in,
    ginp_out, gfilt, gshort,
    inp, go, filt, sw, fwd, bwd, ginp, s_in, s_out,
    pad, wts, kv, mext, gext, taps, ghead, trail, gspec, mspec, stage, zh, zl,
    etail, etail_in, ehead, ehead_in, egrad, egrad_in,
    part, xs, xr, zs, zr, ys, yr, gs, ag,
    s_fil, r_fil, s_edge, r_edge, s_mix, r_mix, s_gl, r_gl,
    sx, rx, sxs, rxs, sz, rz, sy, ry, sg, rg, sh, rh, sa, ra,
):
    seq = lax.axis_index("seq")
    fs = lax.axis_index("fsdp")
    last = NX * NYH * NZ - 1
    z = lax.rem(seq, NZ)
    yh = lax.rem(seq // NZ, NYH)
    x = seq // (NZ * NYH)
    groups = nf + 1
    rows, width = go.shape
    cw = width // NX
    reach = FILTER_LEN
    size = rows + reach
    half = size // 2
    taps_n = nf * GROUP
    assert taps_n == reach
    owner = z < groups
    has_prev = seq > 0
    has_next = seq < last
    far_z = sorted(range(1, NZ), key=lambda d: abs(2 * d - NZ))
    far_x = sorted(range(1, NX), key=lambda d: abs(2 * d - NX))
    loads = [
        pltpu.make_async_copy(a, b, s_in.at[n])
        for n, (a, b) in enumerate(
            ((inp_in, inp), (go_in, go), (sw_in, sw), (filt_in, filt), (fwd_in, fwd), (bwd_in, bwd))
        )
    ]
    for load in loads:
        load.start()

    def at(ax, ay, az):
        return (ax * NYH + ay) * NZ + az

    def around_x(d):
        return at(lax.rem(x + d, NX), yh, z)

    def around_z(d):
        return at(x, yh, lax.rem(z + d, NZ))

    def around_f(d):
        return lax.rem(fs + d, nf)

    def lanes(c):
        return pl.ds(pl.multiple_of(c * cw, cw), cw)

    across = at(x, 1 - yh, z)

    def remote(src, dst, ssem, rsem, s, f):
        return pltpu.make_async_remote_copy(
            src_ref=src, dst_ref=dst, send_sem=ssem, recv_sem=rsem, device_id=(s, f), device_id_type=MESH
        )

    barrier = pltpu.get_barrier_semaphore()

    def greet(s, f):
        pl.semaphore_signal(barrier, inc=1, device_id=(s, f), device_id_type=MESH)

    pl.when(has_prev)(lambda: greet(seq - 1, fs))
    pl.when(has_next)(lambda: greet(seq + 1, fs))
    for d in range(1, nf):
        greet(seq, around_f(d))
    for d in range(1, NX):
        greet(around_x(d), fs)
    for d in range(1, NZ):
        greet(around_z(d), fs)
    greet(across, fs)
    for f in range(nf):
        pl.when(jnp.logical_or(z != fs, fs != f))(lambda f=f: greet(at(x, yh, fs), f))

    for load in loads[:3]:
        load.wait()

    stage[...] = jnp.zeros_like(stage)
    for i in range(3):
        stage[2 * i:2 * i + 2] = inp[i, rows - GROUP:rows].astype(F32)[GROUP - 2:GROUP]
    etail[...] = stage[...].astype(BF16)
    stage[...] = jnp.zeros_like(stage)
    stage[0:2] = inp[0, 0:GROUP].astype(F32)[0:2]
    stage[2:4] = go[0:GROUP].astype(F32)[0:2]
    ehead[...] = stage[...].astype(BF16)
    for i in range(3):
        wts[3 * i:3 * i + 3] = sw[i].astype(F32)

    def tap(i, j, c):
        return wts[3 * i + j:3 * i + j + 1, lanes(c)]

    def short(i, c, lo, n):
        total = tap(i, 0, c) * pad[c, i, LAG + lo:LAG + lo + n]
        for j in range(1, SHORT_LEN):
            total = total + tap(i, j, c) * pad[c, i, LAG + lo - j:LAG + lo - j + n]
        return total

    def mix(c, lo):
        for b in range(lo, lo + reach, BLOCK):
            k = short(1, c, b, BLOCK)
            v = short(2, c, b, BLOCK)
            kv[c, 0, b:b + BLOCK] = k
            kv[c, 1, b:b + BLOCK] = v
            mext[c, reach + b:reach + b + BLOCK] = (k * v).astype(BF16)

    def tail(c, carry):
        for i in range(3):
            pad[c, i, 0:LAG] = jnp.zeros((LAG, cw), F32)
            for b in range(0, rows, BLOCK):
                pad[c, i, LAG + b:LAG + b + BLOCK] = inp[i, b:b + BLOCK, lanes(c)].astype(F32)
        mix(c, rows - reach)
        for b in range(0, reach, BLOCK):
            ghead[c, b:b + BLOCK] = (go[b:b + BLOCK, lanes(c)].astype(F32) * short(0, c, b, BLOCK)).astype(BF16)
        return carry

    lax.fori_loop(0, NX, tail, 0)

    hearers = jnp.where(z < nf, jnp.where(z == fs, NZ - 1, NZ), 0)
    ends = jnp.where(has_prev, 1, 0) + jnp.where(has_next, 1, 0)
    pl.semaphore_wait(barrier, NX - 1 + NZ - 1 + 1 + nf - 1 + hearers + ends)
    loads[3].wait()

    def tail_edge():
        return remote(etail, etail_in, s_edge.at[0], r_edge.at[0], seq + 1, fs)

    def head_edge():
        return remote(ehead, ehead_in, s_edge.at[1], r_edge.at[1], seq - 1, fs)

    def grad_edge():
        return remote(egrad, egrad_in, s_edge.at[2], r_edge.at[2], seq - 1, fs)

    def mix_copy(c):
        return remote(mext.at[c, pl.ds(rows, reach)], mext.at[c, pl.ds(0, reach)], s_mix.at[c], r_mix.at[c], seq + 1, fs)

    def long_copy(c):
        return remote(ghead.at[c], gext.at[c, pl.ds(rows, reach)], s_gl.at[c], r_gl.at[c], seq - 1, fs)

    def filt_copy(d):
        f = around_f(d)
        src = filt.at[:, pl.ds(pl.multiple_of(f * width, width), width)]
        dst = taps.at[pl.ds(pl.multiple_of(fs * GROUP, GROUP), GROUP)]
        return remote(src, dst, s_fil.at[d - 1], r_fil.at[d - 1], seq, f)

    pl.when(has_next)(lambda: tail_edge().start())
    pl.when(has_prev)(lambda: head_edge().start())
    for d in range(NX):
        pl.when(has_next)(lambda d=d: mix_copy(lax.rem(x + 1 + d, NX)).start())
    for d in range(NX):
        pl.when(has_prev)(lambda d=d: long_copy(lax.rem(x + 1 + d, NX)).start())

    for d in range(1, nf):
        filt_copy(d).start()
    taps[pl.ds(pl.multiple_of(fs * GROUP, GROUP), GROUP)] = filt[:, pl.ds(pl.multiple_of(fs * width, width), width)]

    @pl.when(has_prev)
    def _():
        tail_edge().wait_recv()

    @pl.when(jnp.logical_not(has_prev))
    def _():
        etail_in[...] = jnp.zeros_like(etail_in)
        for c in range(NX):
            mext[c, 0:reach] = jnp.zeros((reach, cw), BF16)

    @pl.when(has_next)
    def _():
        head_edge().wait_recv()

    @pl.when(jnp.logical_not(has_next))
    def _():
        ehead_in[...] = jnp.zeros_like(ehead_in)
        egrad_in[...] = jnp.zeros_like(egrad_in)
        for c in range(NX):
            gext[c, rows:size] = jnp.zeros((reach, cw), BF16)

    def rest(c, carry):
        edge = etail_in[:, lanes(c)].astype(F32)
        for i in range(3):
            pad[c, i, LAG - 2:LAG] = edge[2 * i:2 * i + 2]
        mix(c, 0)
        for b in range(0, rows, BLOCK):
            gext[c, b:b + BLOCK] = (go[b:b + BLOCK, lanes(c)].astype(F32) * short(0, c, b, BLOCK)).astype(BF16)
        return carry

    lax.fori_loop(0, NX, rest, 0)

    for load in loads[4:]:
        load.wait()

    def forward(signal, lo, n):
        both = dot(fwd[:, lo:lo + n], signal)
        return both[:size] + both[size:]

    def backward(row, n):
        both = dot(bwd[row:row + 2 * n], zh[...])
        return both[:n] + (both[n:] + dot(bwd[row:row + n], zl[...]))

    def put(lo, value):
        n = value.shape[0]
        high = value.astype(BF16)
        zh[lo:lo + n] = high
        zl[lo:lo + n] = (value - high.astype(F32)).astype(BF16)

    def product(a, b, c):
        for lo in range(0, half, BLOCK):
            ar, ai = a[c, lo:lo + BLOCK], a[c, half + lo:half + lo + BLOCK]
            br, bi = b[c, lo:lo + BLOCK], b[c, half + lo:half + lo + BLOCK]
            put(lo, ar * br + ai * bi)
            put(half + lo, ai * br - ar * bi)

    def x_copy(d):
        src = (part if LINK == F32 else xs).at[lax.rem(x + 1 + d, NX), pl.ds(0, taps_n)]
        return remote(src, xr.at[d, pl.ds(0, taps_n)], sx.at[d], rx.at[d], around_x(1 + d), fs)

    def xs_copy(d):
        src = (part if LINK == F32 else xs).at[lax.rem(x + 1 + d, NX), pl.ds(taps_n, GROUP)]
        return remote(src, xr.at[d, pl.ds(taps_n, GROUP)], sxs.at[d], rxs.at[d], around_x(1 + d), fs)

    def spectra(c, carry):
        gspec[c] = forward(gext[c, 0:rows], 0, rows)
        mspec[c] = forward(mext[c, reach:size], reach, rows)
        return carry

    lax.fori_loop(0, NX, spectra, 0)

    def cross(d, carry):
        c = lax.rem(x + 1 + d, NX)

        @pl.when(has_prev)
        def _():
            mix_copy(c).wait_recv()

        mspec[c] = mspec[c] + forward(mext[c, 0:reach], 0, reach)
        product(gspec, mspec, c)
        terms = backward(0, reach)
        part[c, 0:taps_n] = terms
        if LINK != F32:
            xs[c, 0:taps_n] = terms.astype(LINK)

        @pl.when(d < NX - 1)
        def _():
            x_copy(d).start()

        return carry

    lax.fori_loop(0, NX, cross, 0)

    for d in range(1, nf):
        filt_copy(d).wait_recv()

    def outputs(d, carry):
        c = lax.rem(x + 1 + d, NX)
        spectrum = forward(taps[:, lanes(c)], 0, reach)

        @pl.when(has_next)
        def _():
            long_copy(c).wait_recv()
            block = gext[c, rows:rows + GROUP].astype(F32)
            edge = ehead_in[:, lanes(c)].astype(F32)
            before = pad[c, 0, LAG + rows - 2:LAG + rows]
            first = tap(0, 0, c) * edge[0:1] + tap(0, 1, c) * before[1:2] + tap(0, 2, c) * before[0:1]
            second = tap(0, 0, c) * edge[1:2] + tap(0, 1, c) * edge[0:1] + tap(0, 2, c) * before[1:2]
            row = lax.broadcasted_iota(jnp.int32, (GROUP, cw), 0)
            block = jnp.where(row == 0, edge[2:3] * first, block)
            block = jnp.where(row == 1, edge[3:4] * second, block)
            gext[c, rows:rows + GROUP] = block.astype(BF16)

        fr, fi = spectrum[:half], spectrum[half:]
        for lo in range(0, half, BLOCK):
            ar, ai = mspec[c, lo:lo + BLOCK], mspec[c, half + lo:half + lo + BLOCK]
            br, bi = fr[lo:lo + BLOCK], fi[lo:lo + BLOCK]
            put(lo, ar * br - ai * bi)
            put(half + lo, ar * bi + ai * br)
        long_out = backward(2 * reach, rows)
        trail[c, 0, 0:rows] = (go[:, lanes(c)].astype(F32) * long_out).astype(BF16).astype(F32)
        gspec[c] = gspec[c] + forward(gext[c, rows:size], rows, reach)
        for lo in range(0, half, BLOCK):
            ar, ai = gspec[c, lo:lo + BLOCK], gspec[c, half + lo:half + lo + BLOCK]
            br, bi = fr[lo:lo + BLOCK], fi[lo:lo + BLOCK]
            put(lo, ar * br + ai * bi)
            put(half + lo, ai * br - ar * bi)
        grad_mixed = backward(2 * reach + 2 * rows, rows)
        trail[c, 1, 0:rows] = (grad_mixed * kv[c, 1]).astype(BF16).astype(F32)
        trail[c, 2, 0:rows] = (grad_mixed * kv[c, 0]).astype(BF16).astype(F32)
        part[c, taps_n:taps_n + GROUP] = jnp.zeros((GROUP, cw), F32)
        for i in range(3):
            sums = [jnp.zeros((8, cw), F32)] * SHORT_LEN
            for b in range(0, rows, BLOCK):
                grads = trail[c, i, b:b + BLOCK]
                for j in range(SHORT_LEN):
                    terms = grads * pad[c, i, LAG + b - j:LAG + b - j + BLOCK]
                    sums[j] = sums[j] + jnp.sum(terms.reshape(BLOCK // 8, 8, cw), axis=0)
            for j in range(SHORT_LEN):
                r = taps_n + 3 * i + j
                part[c, r:r + 1] = jnp.sum(sums[j], axis=0, keepdims=True)
        if LINK != F32:
            xs[c, taps_n:taps_n + GROUP] = part[c, taps_n:taps_n + GROUP].astype(LINK)
        for i in range(3):
            stage[2 * i:2 * i + 2, lanes(c)] = trail[c, i, 0:2]

        @pl.when(d < NX - 1)
        def _():
            xs_copy(d).start()

        return carry

    stage[...] = jnp.zeros_like(stage)
    lax.fori_loop(0, NX, outputs, 0)
    egrad[...] = stage[...].astype(BF16)

    @pl.when(has_prev)
    def _():
        grad_edge().start()

    def z_copy(d):
        return remote(zs.at[lax.rem(z + d, NZ)], zr.at[d - 1], sz.at[d - 1], rz.at[d - 1], around_z(d), fs)

    def y_copy():
        return remote(ys, yr, sy, ry, across, fs)

    def g_copy(d, f):
        return remote(gs, ag.at[x, fs], sg.at[d], rg.at[fs], around_z(d), f)

    def g_landing(f):
        return remote(ag.at[x, f], ag.at[x, f], sg.at[0], rg.at[f], across, fs)

    def h_copy(d):
        return remote(ag.at[x, nf], ag.at[x, nf], sh.at[d - 1], rh, around_z(d), fs)

    def a_copy(d, g):
        return remote(ag.at[x, g], ag.at[x, g], sa.at[d - 1, g], ra.at[d - 1, g], around_x(d), fs)

    def a_landing(d, g):
        back = lax.rem(x + NX - d, NX)
        return remote(ag.at[back, g], ag.at[back, g], sa.at[d - 1, g], ra.at[d - 1, g], around_x(d), fs)

    for d in range(NX - 1):
        x_copy(d).wait_recv()
        xs_copy(d).wait_recv()

    def x_total(g):
        here = pl.ds(pl.multiple_of(g * GROUP, GROUP), GROUP)
        total = part[x, here]
        for e in range(NX - 1):
            total = total + xr[e, here].astype(F32)
        return total

    for d in far_z:
        g = lax.rem(z + d, NZ)

        @pl.when(g < groups)
        def _(d=d, g=g):
            zs[g] = x_total(g).astype(zs.dtype)
            z_copy(d).start()

    @pl.when(has_next)
    def _():
        grad_edge().wait_recv()

    def out_copy(c):
        return pltpu.make_async_copy(ginp.at[:, :, lanes(c)], ginp_out.at[:, :, lanes(c)], s_out.at[c])

    def finish(c, carry):
        edge = egrad_in[:, lanes(c)].astype(F32)
        for i in range(3):
            trail[c, i, rows:rows + 2] = edge[2 * i:2 * i + 2]
            for b in range(0, rows, BLOCK):
                total = tap(i, 0, c) * trail[c, i, b:b + BLOCK]
                for j in range(1, SHORT_LEN):
                    total = total + tap(i, j, c) * trail[c, i, b + j:b + j + BLOCK]
                ginp[i, b:b + BLOCK, lanes(c)] = total.astype(BF16)
        out_copy(c).start()
        return carry

    lax.fori_loop(0, NX, finish, 0)

    @pl.when(owner)
    def _():
        total = x_total(z)
        for d in range(1, NZ):
            z_copy(d).wait_recv()
            total = total + zr[d - 1].astype(F32)
        ys[...] = total
        y_copy().start()
        y_copy().wait_recv()
        piece = (total + yr[...]).astype(ag.dtype)
        y_copy().wait_send()

        @pl.when(z < nf)
        def _():
            gs[...] = piece

            @pl.when(z == fs)
            def _():
                ag[x, fs] = piece

            for d in far_z + [0]:
                pl.when(jnp.logical_or(d != 0, z != fs))(lambda d=d: g_copy(d, z).start())

        @pl.when(z == nf)
        def _():
            ag[x, nf] = piece
            for d in far_z:
                h_copy(d).start()

    for g in range(groups):
        if g < nf:
            pl.when(jnp.logical_or(z != fs, fs != g))(lambda g=g: g_landing(g).wait_recv())
        else:
            pl.when(z != nf)(lambda: h_copy(1).wait_recv())
        for d in far_x:
            a_copy(d, g).start()

    def deliver(c, g):
        if g < nf:
            gfilt[:, pl.ds(pl.multiple_of(g * width + c * cw, cw), cw)] = ag[c, g].astype(F32)
        else:
            for i in range(3):
                gshort[i, :, lanes(c)] = ag[c, g].astype(F32)[3 * i:3 * i + 3]

    for g in range(groups):
        deliver(x, g)
    for g in range(groups):
        for d in range(1, NX):
            a_landing(d, g).wait_recv()
            deliver(lax.rem(x + NX - d, NX), g)

    for d in range(1, nf):
        filt_copy(d).wait_send()
    for d in range(NX - 1):
        x_copy(d).wait_send()
        xs_copy(d).wait_send()

    @pl.when(has_next)
    def _():
        tail_edge().wait_send()

    @pl.when(has_prev)
    def _():
        head_edge().wait_send()
        grad_edge().wait_send()

    for c in range(NX):
        pl.when(has_next)(lambda c=c: mix_copy(c).wait_send())
        pl.when(has_prev)(lambda c=c: long_copy(c).wait_send())
    for c in range(NX):
        out_copy(c).wait()

    for d in range(1, NZ):
        pl.when(lax.rem(z + d, NZ) < groups)(lambda d=d: z_copy(d).wait_send())

    @pl.when(z < nf)
    def _():
        for d in range(NZ):
            pl.when(jnp.logical_or(d != 0, z != fs))(lambda d=d: g_copy(d, z).wait_send())

    @pl.when(z == nf)
    def _():
        for d in range(1, NZ):
            h_copy(d).wait_send()

    for g in range(groups):
        for d in range(1, NX):
            a_copy(d, g).wait_send()


def copy_kernel(n, *refs):
    held, sems_in, sems_out = refs[2 * n:3 * n], refs[3 * n], refs[3 * n + 1]
    parts = []
    for src, dst, via in zip(refs[:n], refs[n:2 * n], held):
        if src.dtype == BF16:
            parts += [(src.at[i], via.at[i], dst.at[i]) for i in range(src.shape[0])]
        else:
            parts.append((src, via, dst))
    into = [pltpu.make_async_copy(a, b, sems_in.at[k]) for k, (a, b, _) in enumerate(parts)]
    out = [pltpu.make_async_copy(b, c, sems_out.at[k]) for k, (_, b, c) in enumerate(parts)]
    for copy in into:
        copy.start()
    for a, b in zip(into, out):
        a.wait()
        b.start()
    for copy in out:
        copy.wait()


def placed(results):
    anywhere = pl.BlockSpec(memory_space=pl.ANY)
    n = len(results)
    return pl.pallas_call(
        functools.partial(copy_kernel, n),
        out_shape=tuple(jax.ShapeDtypeStruct(r.shape, r.dtype) for r in results),
        in_specs=[anywhere] * n,
        out_specs=(anywhere,) * n,
        scratch_shapes=[pltpu.VMEM(r.shape, r.dtype) for r in results] + [pltpu.SemaphoreType.DMA((5,))] * 2,
        compiler_params=pltpu.CompilerParams(vmem_limit_bytes=60 * 1024 * 1024),
    )(*results)


def local(inputs, grad_out, filters, short_weights):
    rows, width = grad_out.shape
    nf = lax.axis_size("fsdp")
    cw = width // NX
    size = rows + FILTER_LEN
    matrix = basis(size)
    fwd = np.concatenate(split(matrix), axis=0)
    inverse = matrix.T * (2.0 / size)
    pieces = (-inverse[rows:], inverse[FILTER_LEN:], inverse[:rows])
    bwd = np.concatenate([half for piece in pieces for half in split(piece)], axis=0)
    part_rows = (nf + 1) * GROUP
    dma = pltpu.SemaphoreType.DMA
    vm = pl.BlockSpec(memory_space=pltpu.VMEM)
    anywhere = pl.BlockSpec(memory_space=pl.ANY)
    results = pl.pallas_call(
        functools.partial(fused_kernel, nf),
        out_shape=(
            jax.ShapeDtypeStruct(inputs.shape, BF16),
            jax.ShapeDtypeStruct((GROUP, nf * width), F32),
            jax.ShapeDtypeStruct((3, SHORT_LEN, width), F32),
        ),
        in_specs=[anywhere] * 6,
        out_specs=(anywhere, vm, vm),
        scratch_shapes=[
            pltpu.VMEM(inputs.shape, BF16),
            pltpu.VMEM(grad_out.shape, BF16),
            pltpu.VMEM(filters.shape, BF16),
            pltpu.VMEM(short_weights.shape, BF16),
            pltpu.VMEM(fwd.shape, BF16),
            pltpu.VMEM(bwd.shape, BF16),
            pltpu.VMEM(inputs.shape, BF16),
            dma((6,)), dma((NX,)),
            pltpu.VMEM((NX, 3, LAG + rows, cw), F32),
            pltpu.VMEM((GROUP, width), F32),
            pltpu.VMEM((NX, 2, rows, cw), F32),
            pltpu.VMEM((NX, size, cw), BF16),
            pltpu.VMEM((NX, size, cw), BF16),
            pltpu.VMEM((FILTER_LEN, width), BF16),
            pltpu.VMEM((NX, FILTER_LEN, cw), BF16),
            pltpu.VMEM((NX, 3, rows + LAG, cw), F32),
            pltpu.VMEM((NX, size, cw), F32),
            pltpu.VMEM((NX, size, cw), F32),
            pltpu.VMEM((GROUP, width), F32),
            pltpu.VMEM((size, cw), BF16),
            pltpu.VMEM((size, cw), BF16),
            *[pltpu.VMEM((GROUP, width), BF16)] * 6,
            pltpu.VMEM((NX, part_rows, cw), F32),
            pltpu.VMEM((NX, part_rows, cw), LINK),
            pltpu.VMEM((NX - 1, part_rows, cw), LINK),
            pltpu.VMEM((NZ, GROUP, cw), LINK),
            pltpu.VMEM((NZ - 1, GROUP, cw), LINK),
            pltpu.VMEM((GROUP, cw), F32),
            pltpu.VMEM((GROUP, cw), F32),
            pltpu.VMEM((GROUP, cw), LINK),
            pltpu.VMEM((NX, nf + 1, GROUP, cw), LINK),
            dma((nf - 1,)), dma((nf - 1,)),
            dma((3,)), dma((3,)),
            dma((NX,)), dma((NX,)),
            dma((NX,)), dma((NX,)),
            dma((NX - 1,)), dma((NX - 1,)),
            dma((NX - 1,)), dma((NX - 1,)),
            dma((NZ - 1,)), dma((NZ - 1,)),
            dma, dma,
            dma((NZ,)), dma((nf,)),
            dma((NZ - 1,)), dma,
            dma((NX - 1, nf + 1)), dma((NX - 1, nf + 1)),
        ],
        compiler_params=pltpu.CompilerParams(
            collective_id=0, has_side_effects=True, vmem_limit_bytes=56 * 1024 * 1024
        ),
    )(inputs, grad_out, filters, short_weights, fwd, bwd)
    return placed(results)


def solution(mesh):
    placed = (P(None, "seq", "fsdp"), P("seq", "fsdp"), P("fsdp", None), P(None, None, "fsdp"))
    return jax.shard_map(
        local,
        mesh=mesh,
        in_specs=placed,
        out_specs=(P(None, "seq", "fsdp"), P("fsdp", None), P(None, None, "fsdp")),
        check_vma=False,
    )
```

```python
import functools

import jax
import jax.numpy as jnp
import numpy as np
from jax import lax
from jax.experimental import pallas as pl
from jax.experimental.pallas import tpu as pltpu
from jax.sharding import PartitionSpec as P

FILTER_LEN = 128
SHORT_LEN = 3
NX, NYH, NZ = 4, 2, 12
GROUP = 16
LAG = 8
BLOCK = 32
LINK = jnp.bfloat16
MESH = pl.DeviceIdType.MESH
F32, BF16 = jnp.float32, jnp.bfloat16


def basis(length):
    k = np.arange(length // 2, dtype=np.int64)[:, None]
    t = np.arange(length, dtype=np.int64)[None, :]
    angle = np.pi * (((2 * k + 1) * t) % (2 * length)) / length
    return np.concatenate([np.cos(angle), -np.sin(angle)], axis=0)


def split(matrix):
    high = matrix.astype(jnp.bfloat16)
    low = (matrix - high.astype(np.float64)).astype(jnp.bfloat16)
    return high, low


def dot(a, b):
    return jnp.dot(a, b, preferred_element_type=F32)


def fused_kernel(
    nf, inp_in, go_in, filt_in, sw_in, fwd_in, bwd_in,
    ginp, gfilt, gshort,
    inp, go, filt, sw, fwd, bwd, s_in,
    pad, wts, kv, mext, gext, taps, ghead, trail, gspec, mspec, stage, zh, zl,
    etail, etail_in, ehead, ehead_in, egrad, egrad_in,
    part, xs, xr, zs, zr, ys, yr, gs, ag,
    s_fil, r_fil, s_edge, r_edge, s_mix, r_mix, s_gl, r_gl,
    sx, rx, sxs, rxs, sz, rz, sy, ry, sg, rg, sh, rh, sa, ra,
):
    seq = lax.axis_index("seq")
    fs = lax.axis_index("fsdp")
    last = NX * NYH * NZ - 1
    z = lax.rem(seq, NZ)
    yh = lax.rem(seq // NZ, NYH)
    x = seq // (NZ * NYH)
    groups = nf + 1
    rows, width = go.shape
    cw = width // NX
    reach = FILTER_LEN
    size = rows + reach
    half = size // 2
    taps_n = nf * GROUP
    assert taps_n == reach
    owner = z < groups
    has_prev = seq > 0
    has_next = seq < last
    far_z = sorted(range(1, NZ), key=lambda d: abs(2 * d - NZ))
    far_x = sorted(range(1, NX), key=lambda d: abs(2 * d - NX))
    loads = [
        pltpu.make_async_copy(a, b, s_in.at[n])
        for n, (a, b) in enumerate(
            ((inp_in, inp), (go_in, go), (sw_in, sw), (filt_in, filt), (fwd_in, fwd), (bwd_in, bwd))
        )
    ]
    for load in loads:
        load.start()

    def at(ax, ay, az):
        return (ax * NYH + ay) * NZ + az

    def around_x(d):
        return at(lax.rem(x + d, NX), yh, z)

    def around_z(d):
        return at(x, yh, lax.rem(z + d, NZ))

    def around_f(d):
        return lax.rem(fs + d, nf)

    def lanes(c):
        return pl.ds(pl.multiple_of(c * cw, cw), cw)

    across = at(x, 1 - yh, z)

    def remote(src, dst, ssem, rsem, s, f):
        return pltpu.make_async_remote_copy(
            src_ref=src, dst_ref=dst, send_sem=ssem, recv_sem=rsem, device_id=(s, f), device_id_type=MESH
        )

    barrier = pltpu.get_barrier_semaphore()

    def greet(s, f):
        pl.semaphore_signal(barrier, inc=1, device_id=(s, f), device_id_type=MESH)

    pl.when(has_prev)(lambda: greet(seq - 1, fs))
    pl.when(has_next)(lambda: greet(seq + 1, fs))
    for d in range(1, nf):
        greet(seq, around_f(d))
    for d in range(1, NX):
        greet(around_x(d), fs)
    for d in range(1, NZ):
        greet(around_z(d), fs)
    greet(across, fs)
    for f in range(nf):
        pl.when(jnp.logical_or(z != fs, fs != f))(lambda f=f: greet(at(x, yh, fs), f))

    for load in loads[:3]:
        load.wait()

    stage[...] = jnp.zeros_like(stage)
    for i in range(3):
        stage[2 * i:2 * i + 2] = inp[i, rows - GROUP:rows].astype(F32)[GROUP - 2:GROUP]
    etail[...] = stage[...].astype(BF16)
    stage[...] = jnp.zeros_like(stage)
    stage[0:2] = inp[0, 0:GROUP].astype(F32)[0:2]
    stage[2:4] = go[0:GROUP].astype(F32)[0:2]
    ehead[...] = stage[...].astype(BF16)
    for i in range(3):
        wts[3 * i:3 * i + 3] = sw[i].astype(F32)

    def tap(i, j, c):
        return wts[3 * i + j:3 * i + j + 1, lanes(c)]

    def short(i, c, lo, n):
        total = tap(i, 0, c) * pad[c, i, LAG + lo:LAG + lo + n]
        for j in range(1, SHORT_LEN):
            total = total + tap(i, j, c) * pad[c, i, LAG + lo - j:LAG + lo - j + n]
        return total

    def mix(c, lo):
        for b in range(lo, lo + reach, BLOCK):
            k = short(1, c, b, BLOCK)
            v = short(2, c, b, BLOCK)
            kv[c, 0, b:b + BLOCK] = k
            kv[c, 1, b:b + BLOCK] = v
            mext[c, reach + b:reach + b + BLOCK] = (k * v).astype(BF16)

    def tail(c, carry):
        for i in range(3):
            pad[c, i, 0:LAG] = jnp.zeros((LAG, cw), F32)
            for b in range(0, rows, BLOCK):
                pad[c, i, LAG + b:LAG + b + BLOCK] = inp[i, b:b + BLOCK, lanes(c)].astype(F32)
        mix(c, rows - reach)
        for b in range(0, reach, BLOCK):
            ghead[c, b:b + BLOCK] = (go[b:b + BLOCK, lanes(c)].astype(F32) * short(0, c, b, BLOCK)).astype(BF16)
        return carry

    lax.fori_loop(0, NX, tail, 0)

    hearers = jnp.where(z < nf, jnp.where(z == fs, NZ - 1, NZ), 0)
    ends = jnp.where(has_prev, 1, 0) + jnp.where(has_next, 1, 0)
    pl.semaphore_wait(barrier, NX - 1 + NZ - 1 + 1 + nf - 1 + hearers + ends)
    loads[3].wait()

    def tail_edge():
        return remote(etail, etail_in, s_edge.at[0], r_edge.at[0], seq + 1, fs)

    def head_edge():
        return remote(ehead, ehead_in, s_edge.at[1], r_edge.at[1], seq - 1, fs)

    def grad_edge():
        return remote(egrad, egrad_in, s_edge.at[2], r_edge.at[2], seq - 1, fs)

    def mix_copy(c):
        return remote(mext.at[c, pl.ds(rows, reach)], mext.at[c, pl.ds(0, reach)], s_mix.at[c], r_mix.at[c], seq + 1, fs)

    def long_copy(c):
        return remote(ghead.at[c], gext.at[c, pl.ds(rows, reach)], s_gl.at[c], r_gl.at[c], seq - 1, fs)

    def filt_copy(d):
        f = around_f(d)
        src = filt.at[:, pl.ds(pl.multiple_of(f * width, width), width)]
        dst = taps.at[pl.ds(pl.multiple_of(fs * GROUP, GROUP), GROUP)]
        return remote(src, dst, s_fil.at[d - 1], r_fil.at[d - 1], seq, f)

    pl.when(has_next)(lambda: tail_edge().start())
    pl.when(has_prev)(lambda: head_edge().start())
    for d in range(NX):
        pl.when(has_next)(lambda d=d: mix_copy(lax.rem(x + 1 + d, NX)).start())
    for d in range(NX):
        pl.when(has_prev)(lambda d=d: long_copy(lax.rem(x + 1 + d, NX)).start())

    for d in range(1, nf):
        filt_copy(d).start()
    taps[pl.ds(pl.multiple_of(fs * GROUP, GROUP), GROUP)] = filt[:, pl.ds(pl.multiple_of(fs * width, width), width)]

    @pl.when(has_prev)
    def _():
        tail_edge().wait_recv()

    @pl.when(jnp.logical_not(has_prev))
    def _():
        etail_in[...] = jnp.zeros_like(etail_in)
        for c in range(NX):
            mext[c, 0:reach] = jnp.zeros((reach, cw), BF16)

    @pl.when(has_next)
    def _():
        head_edge().wait_recv()

    @pl.when(jnp.logical_not(has_next))
    def _():
        ehead_in[...] = jnp.zeros_like(ehead_in)
        egrad_in[...] = jnp.zeros_like(egrad_in)
        for c in range(NX):
            gext[c, rows:size] = jnp.zeros((reach, cw), BF16)

    def rest(c, carry):
        edge = etail_in[:, lanes(c)].astype(F32)
        for i in range(3):
            pad[c, i, LAG - 2:LAG] = edge[2 * i:2 * i + 2]
        mix(c, 0)
        for b in range(0, rows, BLOCK):
            gext[c, b:b + BLOCK] = (go[b:b + BLOCK, lanes(c)].astype(F32) * short(0, c, b, BLOCK)).astype(BF16)
        return carry

    lax.fori_loop(0, NX, rest, 0)

    for load in loads[4:]:
        load.wait()

    def forward(signal, lo, n):
        both = dot(fwd[:, lo:lo + n], signal)
        return both[:size] + both[size:]

    def backward(row, n):
        both = dot(bwd[row:row + 2 * n], zh[...])
        return both[:n] + (both[n:] + dot(bwd[row:row + n], zl[...]))

    def put(lo, value):
        n = value.shape[0]
        high = value.astype(BF16)
        zh[lo:lo + n] = high
        zl[lo:lo + n] = (value - high.astype(F32)).astype(BF16)

    def product(a, b, c):
        for lo in range(0, half, BLOCK):
            ar, ai = a[c, lo:lo + BLOCK], a[c, half + lo:half + lo + BLOCK]
            br, bi = b[c, lo:lo + BLOCK], b[c, half + lo:half + lo + BLOCK]
            put(lo, ar * br + ai * bi)
            put(half + lo, ai * br - ar * bi)

    def x_copy(d):
        src = (part if LINK == F32 else xs).at[lax.rem(x + 1 + d, NX), pl.ds(0, taps_n)]
        return remote(src, xr.at[d, pl.ds(0, taps_n)], sx.at[d], rx.at[d], around_x(1 + d), fs)

    def xs_copy(d):
        src = (part if LINK == F32 else xs).at[lax.rem(x + 1 + d, NX), pl.ds(taps_n, GROUP)]
        return remote(src, xr.at[d, pl.ds(taps_n, GROUP)], sxs.at[d], rxs.at[d], around_x(1 + d), fs)

    def spectra(c, carry):
        gspec[c] = forward(gext[c, 0:rows], 0, rows)
        mspec[c] = forward(mext[c, reach:size], reach, rows)
        return carry

    lax.fori_loop(0, NX, spectra, 0)

    def cross(d, carry):
        c = lax.rem(x + 1 + d, NX)

        @pl.when(has_prev)
        def _():
            mix_copy(c).wait_recv()

        mspec[c] = mspec[c] + forward(mext[c, 0:reach], 0, reach)
        product(gspec, mspec, c)
        terms = backward(0, reach)
        part[c, 0:taps_n] = terms
        if LINK != F32:
            xs[c, 0:taps_n] = terms.astype(LINK)

        @pl.when(d < NX - 1)
        def _():
            x_copy(d).start()

        return carry

    lax.fori_loop(0, NX, cross, 0)

    for d in range(1, nf):
        filt_copy(d).wait_recv()

    def outputs(d, carry):
        c = lax.rem(x + 1 + d, NX)
        spectrum = forward(taps[:, lanes(c)], 0, reach)

        @pl.when(has_next)
        def _():
            long_copy(c).wait_recv()
            block = gext[c, rows:rows + GROUP].astype(F32)
            edge = ehead_in[:, lanes(c)].astype(F32)
            before = pad[c, 0, LAG + rows - 2:LAG + rows]
            first = tap(0, 0, c) * edge[0:1] + tap(0, 1, c) * before[1:2] + tap(0, 2, c) * before[0:1]
            second = tap(0, 0, c) * edge[1:2] + tap(0, 1, c) * edge[0:1] + tap(0, 2, c) * before[1:2]
            row = lax.broadcasted_iota(jnp.int32, (GROUP, cw), 0)
            block = jnp.where(row == 0, edge[2:3] * first, block)
            block = jnp.where(row == 1, edge[3:4] * second, block)
            gext[c, rows:rows + GROUP] = block.astype(BF16)

        fr, fi = spectrum[:half], spectrum[half:]
        for lo in range(0, half, BLOCK):
            ar, ai = mspec[c, lo:lo + BLOCK], mspec[c, half + lo:half + lo + BLOCK]
            br, bi = fr[lo:lo + BLOCK], fi[lo:lo + BLOCK]
            put(lo, ar * br - ai * bi)
            put(half + lo, ar * bi + ai * br)
        long_out = backward(2 * reach, rows)
        trail[c, 0, 0:rows] = (go[:, lanes(c)].astype(F32) * long_out).astype(BF16).astype(F32)
        gspec[c] = gspec[c] + forward(gext[c, rows:size], rows, reach)
        for lo in range(0, half, BLOCK):
            ar, ai = gspec[c, lo:lo + BLOCK], gspec[c, half + lo:half + lo + BLOCK]
            br, bi = fr[lo:lo + BLOCK], fi[lo:lo + BLOCK]
            put(lo, ar * br + ai * bi)
            put(half + lo, ai * br - ar * bi)
        grad_mixed = backward(2 * reach + 2 * rows, rows)
        trail[c, 1, 0:rows] = (grad_mixed * kv[c, 1]).astype(BF16).astype(F32)
        trail[c, 2, 0:rows] = (grad_mixed * kv[c, 0]).astype(BF16).astype(F32)
        part[c, taps_n:taps_n + GROUP] = jnp.zeros((GROUP, cw), F32)
        for i in range(3):
            sums = [jnp.zeros((8, cw), F32)] * SHORT_LEN
            for b in range(0, rows, BLOCK):
                grads = trail[c, i, b:b + BLOCK]
                for j in range(SHORT_LEN):
                    terms = grads * pad[c, i, LAG + b - j:LAG + b - j + BLOCK]
                    sums[j] = sums[j] + jnp.sum(terms.reshape(BLOCK // 8, 8, cw), axis=0)
            for j in range(SHORT_LEN):
                r = taps_n + 3 * i + j
                part[c, r:r + 1] = jnp.sum(sums[j], axis=0, keepdims=True)
        if LINK != F32:
            xs[c, taps_n:taps_n + GROUP] = part[c, taps_n:taps_n + GROUP].astype(LINK)
        for i in range(3):
            stage[2 * i:2 * i + 2, lanes(c)] = trail[c, i, 0:2]

        @pl.when(d < NX - 1)
        def _():
            xs_copy(d).start()

        return carry

    stage[...] = jnp.zeros_like(stage)
    lax.fori_loop(0, NX, outputs, 0)
    egrad[...] = stage[...].astype(BF16)

    @pl.when(has_prev)
    def _():
        grad_edge().start()

    def z_copy(d):
        return remote(zs.at[lax.rem(z + d, NZ)], zr.at[d - 1], sz.at[d - 1], rz.at[d - 1], around_z(d), fs)

    def y_copy():
        return remote(ys, yr, sy, ry, across, fs)

    def g_copy(d, f):
        return remote(gs, ag.at[x, fs], sg.at[d], rg.at[fs], around_z(d), f)

    def g_landing(f):
        return remote(ag.at[x, f], ag.at[x, f], sg.at[0], rg.at[f], across, fs)

    def h_copy(d):
        return remote(ag.at[x, nf], ag.at[x, nf], sh.at[d - 1], rh, around_z(d), fs)

    def a_copy(d, g):
        return remote(ag.at[x, g], ag.at[x, g], sa.at[d - 1, g], ra.at[d - 1, g], around_x(d), fs)

    def a_landing(d, g):
        back = lax.rem(x + NX - d, NX)
        return remote(ag.at[back, g], ag.at[back, g], sa.at[d - 1, g], ra.at[d - 1, g], around_x(d), fs)

    for d in range(NX - 1):
        x_copy(d).wait_recv()
        xs_copy(d).wait_recv()

    def x_total(g):
        here = pl.ds(pl.multiple_of(g * GROUP, GROUP), GROUP)
        total = part[x, here]
        for e in range(NX - 1):
            total = total + xr[e, here].astype(F32)
        return total

    for d in far_z:
        g = lax.rem(z + d, NZ)

        @pl.when(g < groups)
        def _(d=d, g=g):
            zs[g] = x_total(g).astype(zs.dtype)
            z_copy(d).start()

    @pl.when(has_next)
    def _():
        grad_edge().wait_recv()

    def finish(c, carry):
        edge = egrad_in[:, lanes(c)].astype(F32)
        for i in range(3):
            trail[c, i, rows:rows + 2] = edge[2 * i:2 * i + 2]
            for b in range(0, rows, BLOCK):
                total = tap(i, 0, c) * trail[c, i, b:b + BLOCK]
                for j in range(1, SHORT_LEN):
                    total = total + tap(i, j, c) * trail[c, i, b + j:b + j + BLOCK]
                ginp[i, b:b + BLOCK, lanes(c)] = total.astype(BF16)
        return carry

    lax.fori_loop(0, NX, finish, 0)

    @pl.when(owner)
    def _():
        total = x_total(z)
        for d in range(1, NZ):
            z_copy(d).wait_recv()
            total = total + zr[d - 1].astype(F32)
        ys[...] = total
        y_copy().start()
        y_copy().wait_recv()
        piece = (total + yr[...]).astype(ag.dtype)
        y_copy().wait_send()

        @pl.when(z < nf)
        def _():
            gs[...] = piece

            @pl.when(z == fs)
            def _():
                ag[x, fs] = piece

            for d in far_z + [0]:
                pl.when(jnp.logical_or(d != 0, z != fs))(lambda d=d: g_copy(d, z).start())

        @pl.when(z == nf)
        def _():
            ag[x, nf] = piece
            for d in far_z:
                h_copy(d).start()

    for g in range(groups):
        if g < nf:
            pl.when(jnp.logical_or(z != fs, fs != g))(lambda g=g: g_landing(g).wait_recv())
        else:
            pl.when(z != nf)(lambda: h_copy(1).wait_recv())
        for d in far_x:
            a_copy(d, g).start()

    def deliver(c, g):
        if g < nf:
            gfilt[:, pl.ds(pl.multiple_of(g * width + c * cw, cw), cw)] = ag[c, g].astype(F32)
        else:
            for i in range(3):
                gshort[i, :, lanes(c)] = ag[c, g].astype(F32)[3 * i:3 * i + 3]

    for g in range(groups):
        deliver(x, g)
    for g in range(groups):
        for d in range(1, NX):
            a_landing(d, g).wait_recv()
            deliver(lax.rem(x + NX - d, NX), g)

    for d in range(1, nf):
        filt_copy(d).wait_send()
    for d in range(NX - 1):
        x_copy(d).wait_send()
        xs_copy(d).wait_send()

    @pl.when(has_next)
    def _():
        tail_edge().wait_send()

    @pl.when(has_prev)
    def _():
        head_edge().wait_send()
        grad_edge().wait_send()

    for c in range(NX):
        pl.when(has_next)(lambda c=c: mix_copy(c).wait_send())
        pl.when(has_prev)(lambda c=c: long_copy(c).wait_send())

    for d in range(1, NZ):
        pl.when(lax.rem(z + d, NZ) < groups)(lambda d=d: z_copy(d).wait_send())

    @pl.when(z < nf)
    def _():
        for d in range(NZ):
            pl.when(jnp.logical_or(d != 0, z != fs))(lambda d=d: g_copy(d, z).wait_send())

    @pl.when(z == nf)
    def _():
        for d in range(1, NZ):
            h_copy(d).wait_send()

    for g in range(groups):
        for d in range(1, NX):
            a_copy(d, g).wait_send()


def local(inputs, grad_out, filters, short_weights):
    rows, width = grad_out.shape
    nf = lax.axis_size("fsdp")
    cw = width // NX
    size = rows + FILTER_LEN
    matrix = basis(size)
    fwd = np.concatenate(split(matrix), axis=0)
    inverse = matrix.T * (2.0 / size)
    pieces = (-inverse[rows:], inverse[FILTER_LEN:], inverse[:rows])
    bwd = np.concatenate([half for piece in pieces for half in split(piece)], axis=0)
    part_rows = (nf + 1) * GROUP
    dma = pltpu.SemaphoreType.DMA
    vm = pl.BlockSpec(memory_space=pltpu.VMEM)
    anywhere = pl.BlockSpec(memory_space=pl.ANY)
    results = pl.pallas_call(
        functools.partial(fused_kernel, nf),
        out_shape=(
            pltpu.VMEM(inputs.shape, BF16),
            pltpu.VMEM((GROUP, nf * width), F32),
            pltpu.VMEM((3, SHORT_LEN, width), F32),
        ),
        in_specs=[anywhere] * 6,
        out_specs=(vm, vm, vm),
        scratch_shapes=[
            pltpu.VMEM(inputs.shape, BF16),
            pltpu.VMEM(grad_out.shape, BF16),
            pltpu.VMEM(filters.shape, BF16),
            pltpu.VMEM(short_weights.shape, BF16),
            pltpu.VMEM(fwd.shape, BF16),
            pltpu.VMEM(bwd.shape, BF16),
            dma((6,)),
            pltpu.VMEM((NX, 3, LAG + rows, cw), F32),
            pltpu.VMEM((GROUP, width), F32),
            pltpu.VMEM((NX, 2, rows, cw), F32),
            pltpu.VMEM((NX, size, cw), BF16),
            pltpu.VMEM((NX, size, cw), BF16),
            pltpu.VMEM((FILTER_LEN, width), BF16),
            pltpu.VMEM((NX, FILTER_LEN, cw), BF16),
            pltpu.VMEM((NX, 3, rows + LAG, cw), F32),
            pltpu.VMEM((NX, size, cw), F32),
            pltpu.VMEM((NX, size, cw), F32),
            pltpu.VMEM((GROUP, width), F32),
            pltpu.VMEM((size, cw), BF16),
            pltpu.VMEM((size, cw), BF16),
            *[pltpu.VMEM((GROUP, width), BF16)] * 6,
            pltpu.VMEM((NX, part_rows, cw), F32),
            pltpu.VMEM((NX, part_rows, cw), LINK),
            pltpu.VMEM((NX - 1, part_rows, cw), LINK),
            pltpu.VMEM((NZ, GROUP, cw), LINK),
            pltpu.VMEM((NZ - 1, GROUP, cw), LINK),
            pltpu.VMEM((GROUP, cw), F32),
            pltpu.VMEM((GROUP, cw), F32),
            pltpu.VMEM((GROUP, cw), LINK),
            pltpu.VMEM((NX, nf + 1, GROUP, cw), LINK),
            dma((nf - 1,)), dma((nf - 1,)),
            dma((3,)), dma((3,)),
            dma((NX,)), dma((NX,)),
            dma((NX,)), dma((NX,)),
            dma((NX - 1,)), dma((NX - 1,)),
            dma((NX - 1,)), dma((NX - 1,)),
            dma((NZ - 1,)), dma((NZ - 1,)),
            dma, dma,
            dma((NZ,)), dma((nf,)),
            dma((NZ - 1,)), dma,
            dma((NX - 1, nf + 1)), dma((NX - 1, nf + 1)),
        ],
        compiler_params=pltpu.CompilerParams(
            collective_id=0, has_side_effects=True, vmem_limit_bytes=56 * 1024 * 1024
        ),
    )(inputs, grad_out, filters, short_weights, fwd, bwd)
    return tuple(results)


def solution(mesh):
    placed = (P(None, "seq", "fsdp"), P("seq", "fsdp"), P("fsdp", None), P(None, None, "fsdp"))
    return jax.shard_map(
        local,
        mesh=mesh,
        in_specs=placed,
        out_specs=(P(None, "seq", "fsdp"), P("fsdp", None), P(None, None, "fsdp")),
        check_vma=False,
    )
```
